32 devices in a mesh: groups: 2 (over x), tile: 16 (over z, y, core).
Axes of the slice: x: 2, y: 2, z: 4, core: 2. Of those that a mesh axis runs over, the one named last changes fastest.
Arguments:
- grid_latent: bfloat16 [32768, 512], P(('groups', 'tile')), parts along dimension 0, may hold values from -6 to 6
- mesh_latent: bfloat16 [8192, 512], P(('groups', 'tile')), parts along dimension 0, may hold values from -6 to 6
- enc_feats: float32 [4, 65536], P(None, ('groups', 'tile')), parts along dimension 1, may hold values from -6 to 6
- enc_sender: int32 [65536], P(('groups', 'tile')), parts along dimension 0, may hold values from 0 to 1535, as said below
- enc_receiver: int32 [65536], P(('groups', 'tile')), parts along dimension 0, may hold values from 0 to 255
- enc_count: int32 [32], P(('groups', 'tile')), parts along dimension 0, may hold values from 1024 to 2048
- mesh_feats: float32 [4, 65536], P(None, ('groups', 'tile')), parts along dimension 1, may hold values from -6 to 6
- mesh_sender: int32 [65536], P(('groups', 'tile')), parts along dimension 0, may hold values from 0 to 255, as said below
- mesh_receiver: int32 [65536], P(('groups', 'tile')), parts along dimension 0, may hold values from 0 to 255
- mesh_count: int32 [32], P(('groups', 'tile')), parts along dimension 0, may hold values from 1024 to 2048
- need_rows: int32 [32, 16, 16], P(('groups', 'tile')), parts along dimension 0, may hold values from 0 to 255, as said below
- w_enc_feat: float32 [4, 512], replicated, may hold values from -3 to 3
- w_enc_send: bfloat16 [512, 512], replicated, may hold values from -0.25 to 0.25
- w_enc_recv: bfloat16 [512, 512], replicated, may hold values from -0.25 to 0.25
- w_enc_out: bfloat16 [512, 512], replicated, may hold values from -0.25 to 0.25
- w_enc_node_in: bfloat16 [1024, 512], replicated, may hold values from -0.1875 to 0.1875
- w_enc_node_out: bfloat16 [512, 512], replicated, may hold values from -0.25 to 0.25
- w_proc_feat: float32 [4, 512], replicated, may hold values from -3 to 3
- w_proc_send: bfloat16 [512, 512], replicated, may hold values from -0.25 to 0.25
- w_proc_recv: bfloat16 [512, 512], replicated, may hold values from -0.25 to 0.25
- w_proc_out: bfloat16 [512, 512], replicated, may hold values from -0.25 to 0.25
- w_proc_node_in: bfloat16 [1024, 512], replicated, may hold values from -0.1875 to 0.1875
- w_proc_node_out: bfloat16 [512, 512], replicated, may hold values from -0.25 to 0.25
Outputs:
- mesh_out: bfloat16 [8192, 512], P(('groups', 'tile')), parts along dimension 0
The draws below stay inside these ranges and needn't reach their ends.
There are 2 independent parts, one for each index of `groups`. The reference program is written for one: setup_inputs(seed, part) draws one part's arguments, and reference() takes and returns one part's arrays. A program takes and returns all parts, laid end to end along the dimension named above; an argument that names none is the same for every part. Nothing has to cross between parts.
Inputs may be any that keep to these rules, and one draw needn't show every extreme that they name: `enc_sender`: in block 0 every entry is 256 or more, in the last block every entry is under 1024 + 256; so no edge starts outside the grid. `mesh_sender`: entry p * 16 + s names need_rows[b, p, s] of the slot's own block b. `need_rows`: the 16 entries of each list are distinct.
All inputs are finite; a program needn't handle non-finite values.
Results may differ from the reference program's by a relative error of at most 0.009.
Values may be sent and summed in bfloat16 or wider, within the bound.
No kernel may reach another device: no remote copies, remote signals or barrier semaphores. Data moves between devices by JAX's collectives and lax.ppermute only.
A program may use at most 64 MiB of HBM per device.

```python
import jax
import jax.numpy as jnp
from jax import lax

D = 512
G_DEV = 1024
HALO = 256
M_DEV = 256
CAP = 16
E_ENC = 2048
M_EDGES = 2048
GRID = 16384
MESH = 4096
ENC_ALL = 32768
MESH_ALL = 32768
N_TILE = 16


def live_counts(key, most):
    counts = jax.random.randint(key, (N_TILE,), most // 2, most + 1)
    full = jax.random.randint(jax.random.fold_in(key, 11), (), 0, N_TILE)
    return counts.at[full].set(most).astype(jnp.int32)


def draw_enc_count(key, part):
    key = jax.random.fold_in(key, 1)
    return live_counts(key, E_ENC)


def draw_mesh_count(key, part):
    key = jax.random.fold_in(key, 2)
    return live_counts(key, M_EDGES)


def draw_enc_sender(key, part):
    key = jax.random.fold_in(key, 3)
    block = jnp.arange(N_TILE, dtype=jnp.int32)[:, None]
    lower = jnp.where(block == 0, HALO, 0)
    upper = jnp.where(block == N_TILE - 1, G_DEV + HALO, G_DEV + 2 * HALO)
    raw = jax.random.randint(key, (N_TILE, E_ENC), 0, 2 ** 24)
    rows = lower + raw % (upper - lower)
    rows = rows.at[:, 0].set(lower[:, 0])
    rows = rows.at[:, 1].set(upper[:, 0] - 1)
    return rows.reshape(-1).astype(jnp.int32)


def draw_mesh_sender(key, part):
    key = jax.random.fold_in(key, 5)
    block = jnp.arange(N_TILE, dtype=jnp.int32)[:, None]
    peer = jax.random.randint(jax.random.fold_in(key, 1), (N_TILE, M_EDGES), 0, N_TILE)
    local = jax.random.randint(jax.random.fold_in(key, 2), (N_TILE, M_EDGES), 0, 2) == 0
    peer = jnp.where(local, block, peer)
    column = jnp.arange(M_EDGES, dtype=jnp.int32)[None, :]
    peer = jnp.where(column < N_TILE, column, peer)
    slot = jax.random.randint(jax.random.fold_in(key, 3), (N_TILE, M_EDGES), 0, CAP)
    entry = peer * CAP + slot
    entry = entry.at[:, 0].set(0)
    entry = entry.at[:, N_TILE - 1].set(N_TILE * CAP - 1)
    return entry.reshape(-1).astype(jnp.int32)


def draw_need_rows(key, part):
    key = jax.random.fold_in(key, 7)
    scores = jax.random.randint(key, (N_TILE, N_TILE, M_DEV), 0, 2 ** 30)
    order = jnp.argsort(scores, axis=-1)
    return order[:, :, :CAP].astype(jnp.int32)


def with_ends(values, stream_key, least, top_value):
    extent = values.shape
    spot = [jax.random.randint(jax.random.fold_in(stream_key, axis), (), 0, extent[axis]) for axis in range(len(extent))]
    values = values.at[tuple(spot)].set(least)
    longest = extent.index(max(extent))
    spot[longest] = (spot[longest] + 1) % extent[longest]
    return values.at[tuple(spot)].set(top_value)


def steps_of(stream_key, shape, split, smallest, largest):
    factor_of, own = 1.0, jax.random.fold_in(stream_key, 6)
    for axis_at, blocks in split:
        steps = jnp.exp(jax.random.uniform(jax.random.fold_in(own, axis_at), (blocks,), jnp.float32, smallest / len(split), largest / len(split)))
        factor_of = factor_of * jnp.repeat(steps, shape[axis_at] // blocks).reshape([-1 if axis == axis_at else 1 for axis in range(len(shape))])
    return factor_of


def gaussian(own_key, shape, scale, most, cuts=(), held_as=jnp.bfloat16):
    values = jax.random.normal(own_key, shape, jnp.float32) * scale
    if len(cuts) > 0:
        values = steps_of(own_key, shape, cuts, -0.22, 0.18) * values
    return jnp.clip(values, min=-most, max=most).astype(held_as)


def setup_inputs(seed: int = 0, part: int = 0) -> dict:
    key_of = jax.random.split(jax.random.key(seed), 24)
    part_splits = jax.random.split(jax.random.fold_in(key_of[23], part), 24)
    return {
        "grid_latent": gaussian(part_splits[0], (GRID, D), 1.0, 6.0, ((0, 16),)),
        "mesh_latent": gaussian(part_splits[1], (MESH, D), 1.0, 6.0, ((0, 16),)),
        "enc_feats": gaussian(part_splits[2], (4, ENC_ALL), 1.0, 6.0, ((1, 16),), jnp.float32),
        "enc_sender": draw_enc_sender(jax.random.fold_in(jax.random.fold_in(key_of[23], part), 71), part),
        "enc_receiver": with_ends(jax.random.randint(part_splits[4], (ENC_ALL,), 0, M_DEV), jax.random.fold_in(part_splits[4], 1), 0, M_DEV - 1).astype(jnp.int32),
        "enc_count": draw_enc_count(jax.random.fold_in(jax.random.fold_in(key_of[23], part), 71), part),
        "mesh_feats": gaussian(part_splits[6], (4, MESH_ALL), 1.0, 6.0, ((1, 16),), jnp.float32),
        "mesh_sender": draw_mesh_sender(jax.random.fold_in(jax.random.fold_in(key_of[23], part), 71), part),
        "mesh_receiver": with_ends(jax.random.randint(part_splits[8], (MESH_ALL,), 0, M_DEV), jax.random.fold_in(part_splits[8], 1), 0, M_DEV - 1).astype(jnp.int32),
        "mesh_count": draw_mesh_count(jax.random.fold_in(jax.random.fold_in(key_of[23], part), 71), part),
        "need_rows": draw_need_rows(jax.random.fold_in(jax.random.fold_in(key_of[23], part), 71), part),
        "w_enc_feat": gaussian(key_of[11], (4, D), 4 ** -0.5, 3.0, (), jnp.float32),
        "w_enc_send": gaussian(key_of[12], (D, D), D ** -0.5, 0.25),
        "w_enc_recv": gaussian(key_of[13], (D, D), D ** -0.5, 0.25),
        "w_enc_out": gaussian(key_of[14], (D, D), D ** -0.5, 0.25),
        "w_enc_node_in": gaussian(key_of[15], (2 * D, D), (2 * D) ** -0.5, 0.1875),
        "w_enc_node_out": gaussian(key_of[16], (D, D), D ** -0.5, 0.25),
        "w_proc_feat": gaussian(key_of[17], (4, D), 4 ** -0.5, 3.0, (), jnp.float32),
        "w_proc_send": gaussian(key_of[18], (D, D), D ** -0.5, 0.25),
        "w_proc_recv": gaussian(key_of[19], (D, D), D ** -0.5, 0.25),
        "w_proc_out": gaussian(key_of[20], (D, D), D ** -0.5, 0.25),
        "w_proc_node_in": gaussian(key_of[21], (2 * D, D), (2 * D) ** -0.5, 0.1875),
        "w_proc_node_out": gaussian(key_of[22], (D, D), D ** -0.5, 0.25),
    }


def layer_norm(values):
    mean = lax.optimization_barrier(jnp.mean(values, axis=-1, keepdims=True))
    centered = values - mean
    variance = lax.optimization_barrier(jnp.mean(centered * centered, axis=-1, keepdims=True))
    return centered * lax.rsqrt(variance + 1e-05)

def edge_block(feats, sender_rows, receiver_rows, w_feat, w_out, count):
    base = jnp.einsum('ke,kd->ed', feats, w_feat, precision=lax.Precision.HIGHEST)
    pre = base + sender_rows.astype(jnp.float32) + receiver_rows.astype(jnp.float32)
    hidden = jax.nn.silu(pre).astype(jnp.bfloat16)
    out = layer_norm(jnp.dot(hidden, w_out, preferred_element_type=jnp.float32))
    live = (jnp.arange(feats.shape[1], dtype=jnp.int32) < count).astype(jnp.float32)
    return (out * live[:, None]).astype(jnp.bfloat16)

def aggregate(messages, receivers, nodes):
    onehot = (receivers[None, :] == jnp.arange(nodes, dtype=jnp.int32)[:, None]).astype(jnp.bfloat16)
    return jnp.dot(onehot, messages, preferred_element_type=jnp.float32).astype(jnp.bfloat16)

def node_block(latent, summed, w_in, w_out):
    joined = jnp.concatenate([latent, summed], axis=1)
    hidden = jax.nn.silu(jnp.dot(joined, w_in, preferred_element_type=jnp.float32)).astype(jnp.bfloat16)
    update = layer_norm(jnp.dot(hidden, w_out, preferred_element_type=jnp.float32))
    return (latent.astype(jnp.float32) + update).astype(jnp.bfloat16)

def reference(grid_latent, mesh_latent, enc_feats, enc_sender, enc_receiver, enc_count, mesh_feats, mesh_sender, mesh_receiver, mesh_count, need_rows, w_enc_feat, w_enc_send, w_enc_recv, w_enc_out, w_enc_node_in, w_enc_node_out, w_proc_feat, w_proc_send, w_proc_recv, w_proc_out, w_proc_node_in, w_proc_node_out):
    grid_proj = jnp.dot(grid_latent, w_enc_send, preferred_element_type=jnp.float32).astype(jnp.bfloat16)
    blocks = jnp.arange(N_TILE, dtype=jnp.int32)
    enc_feat_blocks = jnp.transpose(enc_feats.reshape(4, N_TILE, E_ENC), (1, 0, 2))
    latent_blocks = mesh_latent.reshape(N_TILE, M_DEV, D)

    def encode(items):
        block, feats, senders, receivers, count, latent = items
        rows = (senders + block * G_DEV - HALO).astype(jnp.int32)
        sender_rows = jnp.take(grid_proj, rows, axis=0)
        recv_proj = jnp.dot(latent, w_enc_recv, preferred_element_type=jnp.float32).astype(jnp.bfloat16)
        receiver_rows = jnp.take(recv_proj, receivers, axis=0)
        messages = edge_block(feats, sender_rows, receiver_rows, w_enc_feat, w_enc_out, count)
        summed = aggregate(messages, receivers, M_DEV)
        return node_block(latent, summed, w_enc_node_in, w_enc_node_out)
    mesh_mid = lax.map(encode, (blocks, enc_feat_blocks, enc_sender.reshape(N_TILE, E_ENC), enc_receiver.reshape(N_TILE, E_ENC), enc_count, latent_blocks))
    flat_mid = mesh_mid.reshape(N_TILE * M_DEV, D)
    send_proj = jnp.dot(flat_mid, w_proc_send, preferred_element_type=jnp.float32).astype(jnp.bfloat16)
    mesh_feat_blocks = jnp.transpose(mesh_feats.reshape(4, N_TILE, M_EDGES), (1, 0, 2))

    def process(items):
        feats, senders, receivers, count, latent, needed = items
        ids = (jnp.arange(N_TILE, dtype=jnp.int32)[:, None] * M_DEV + needed).reshape(-1).astype(jnp.int32)
        listed = jnp.take(send_proj, ids, axis=0)
        sender_rows = jnp.take(listed, senders, axis=0)
        recv_proj = jnp.dot(latent, w_proc_recv, preferred_element_type=jnp.float32).astype(jnp.bfloat16)
        receiver_rows = jnp.take(recv_proj, receivers, axis=0)
        messages = edge_block(feats, sender_rows, receiver_rows, w_proc_feat, w_proc_out, count)
        summed = aggregate(messages, receivers, M_DEV)
        return node_block(latent, summed, w_proc_node_in, w_proc_node_out)
    result = lax.map(process, (mesh_feat_blocks, mesh_sender.reshape(N_TILE, M_EDGES), mesh_receiver.reshape(N_TILE, M_EDGES), mesh_count, mesh_mid, need_rows))
    return result.reshape(N_TILE * M_DEV, D)
```

```python
import functools

import jax
import jax.numpy as jnp
from jax import lax
from jax.experimental import pallas as pl
from jax.experimental.pallas import tpu as pltpu
from jax.sharding import PartitionSpec as P

HALO = 256
BLOCK = 512
F32, BF16 = jnp.float32, jnp.bfloat16
NN = (((1,), (0,)), ((), ()))
NT = (((1,), (1,)), ((), ()))
TN = (((0,), (0,)), ((), ()))
TT = (((0,), (1,)), ((), ()))


def mul(a, b, dims=NN):
    return lax.dot_general(a, b, dims, preferred_element_type=F32)


def swish(v):
    half = 0.5 * v
    return half * jnp.tanh(half) + half


def norm(x, axis):
    size = x.shape[axis]
    centered = x - jnp.sum(x, axis=axis, keepdims=True) * (1.0 / size)
    variance = jnp.sum(centered * centered, axis=axis, keepdims=True) * (1.0 / size)
    return centered, lax.rsqrt(variance + 1e-05)


def places(rows, indices):
    at = lax.broadcasted_iota(jnp.int32, (rows, indices.shape[1]), 0).astype(jnp.int16)
    one, zero = jnp.array(1, BF16), jnp.array(0, BF16)
    return jnp.where(at == indices.astype(jnp.int16), one, zero)


def split(x):
    high = x.astype(BF16)
    return high, (x - high.astype(F32)).astype(BF16)


def stack_feats(feats, w_feat, fa, wa):
    rows = feats.shape[0]
    fa[...] = jnp.zeros(fa.shape, F32)
    wa[...] = jnp.zeros(wa.shape, F32)
    f_high, f_low = split(feats[...])
    w_high, w_low = split(w_feat[...])
    for at, (f, w) in enumerate(((f_high, w_high), (f_high, w_low), (f_low, w_high))):
        fa[at * rows : (at + 1) * rows, :] = f.astype(F32)
        wa[at * rows : (at + 1) * rows, :] = w.astype(F32)


def fetch(pairs, sems):
    copies = [pltpu.make_async_copy(a, b, sems.at[i]) for i, (a, b) in enumerate(pairs)]
    for copy in copies:
        copy.start()

    def ready(*which):
        for i in which:
            copies[i].wait()

    return ready


def summed_messages(total, pre_of, to_of, w_out, count):
    w_out = w_out[...]
    held = {}

    def first(i):
        return to_of(i), swish(pre_of(i)).astype(BF16)

    def second(i, to, hidden):
        return to, mul(w_out, hidden, TN)

    def third(i, to, out):
        out, scale = norm(out, 0)
        live = lax.broadcasted_iota(jnp.int32, (1, BLOCK), 1) + i * BLOCK < count
        return to, (out * jnp.where(live, scale, 0.0)).astype(BF16)

    def last(i, to, message):
        return (mul(to, message, NT),)

    stages = (first, second, third, last)
    summed = None
    for step in range(total // BLOCK + len(stages) - 1):
        for at, stage in enumerate(stages):
            i = step - at
            if 0 <= i < total // BLOCK:
                held[i] = stage(i, *held.get(i, ()))
                if stage is last:
                    part = held.pop(i)[0]
                    summed = part if summed is None else summed + part
    return summed.astype(BF16)


def nodes_of(latent, summed, w_in, w_out):
    width = latent.shape[1]
    hidden = swish(mul(latent, w_in[:width, :]) + mul(summed, w_in[width:, :])).astype(BF16)
    centered, scale = norm(mul(hidden, w_out[...]), 1)
    return (latent.astype(F32) + centered * scale).astype(BF16)


def in_a_row(asked, rows):
    blocks, _, per = asked.shape
    for i in range(blocks):
        rows[i : i + 1, :] = asked[i].astype(F32)
    size = (per, blocks * per)
    column = lax.broadcasted_iota(jnp.int32, size, 1) % per
    repeat = (column == lax.broadcasted_iota(jnp.int32, size, 0)).astype(F32).astype(BF16)
    wide = mul(rows[...].astype(BF16), repeat)
    size = wide.shape
    block = lax.broadcasted_iota(jnp.int32, size, 1) // per
    own = block == lax.broadcasted_iota(jnp.int32, size, 0)
    return jnp.sum(jnp.where(own, wide, 0.0), axis=0, keepdims=True).astype(jnp.int32)


def band_ends(grid_any, pair_any, other_any, pair, other, sems, out_sems):
    first = (lax.axis_index("tile") % 2) * (grid_any.shape[0] - HALO)
    last = grid_any.shape[0] - HALO - first
    fetch(
        (
            (grid_any.at[pl.ds(pl.multiple_of(last, HALO), HALO), :], pair),
            (grid_any.at[pl.ds(pl.multiple_of(first, HALO), HALO), :], other),
        ),
        sems,
    )(0, 1)
    fetch(((pair, pair_any), (other, other_any)), out_sems)(0, 1)


def encode(
    from_pair, from_other,
    count_any, feats_any, sender_any, receiver_any, feat_any, latent_any, recv_any, send_any,
    grid_any, out_any, in_any, node_any, next_any,
    mid, sent,
    count, feats, sender, receiver, w_feat, latent, w_recv, w_send, grid, w_out, w_in, w_node,
    w_next, table, recv_table, fa, wa, sems,
):
    ready = fetch(
        (
            (feats_any, feats), (feat_any, w_feat), (latent_any, latent), (recv_any, w_recv),
            (send_any, w_send), (grid_any, grid), (sender_any, sender), (receiver_any, receiver),
            (out_any, w_out), (count_any, count), (in_any, w_in), (node_any, w_node),
            (next_any, w_next),
        ),
        sems,
    )
    own = grid.shape[0]
    ready(0, 1)
    stack_feats(feats, w_feat, fa, wa)
    ready(2, 3)
    recv_table[...] = mul(w_recv[...], latent[...], TT).astype(BF16)
    ready(4)
    table[:, :HALO] = mul(w_send[...], from_pair[...], TT).astype(BF16)
    table[:, HALO : 2 * HALO] = mul(w_send[...], from_other[...], TT).astype(BF16)
    ready(5)
    table[:, 2 * HALO :] = mul(w_send[...], grid[...], TT).astype(BF16)
    wab = wa[...].astype(BF16)
    ready(6, 7, 8, 9)
    odd = lax.axis_index("tile") % 2
    above, below = (1 - odd) * HALO, odd * HALO

    def to_of(i):
        return places(recv_table.shape[1], receiver[:, pl.ds(i * BLOCK, BLOCK)])

    def pre_of(i):
        span = pl.ds(i * BLOCK, BLOCK)
        s = sender[:, span]
        s = jnp.where(
            s < HALO,
            s + above,
            jnp.where(s < HALO + own, s + HALO, s - (HALO + own) + below),
        )
        pre = mul(table[...], places(table.shape[1], s))
        pre += mul(recv_table[...], to_of(i))
        return pre + mul(wab, fa[:, span].astype(BF16), TN)

    summed = summed_messages(sender.shape[1], pre_of, to_of, w_out, count[0])
    ready(10, 11, 12)
    middle = nodes_of(latent[...], summed, w_in, w_node)
    mid[...] = middle
    sent[...] = mul(middle, w_next[...]).astype(BF16)


def answer(sent, asked, outgoing_any, outgoing, rows, sems):
    at = places(sent.shape[0], in_a_row(asked, rows))
    outgoing[...] = mul(at, sent[...], TN).astype(BF16)
    fetch(((outgoing, outgoing_any),), sems)(0)


def process_own(
    mid, feats_any, receiver_any, feat_any, recv_any, pre,
    feats, receiver, w_feat, w_recv, recv_table, fa, wa, sems,
):
    ready = fetch(
        (
            (feats_any, feats), (feat_any, w_feat), (recv_any, w_recv), (receiver_any, receiver),
        ),
        sems,
    )
    ready(0, 1)
    stack_feats(feats, w_feat, fa, wa)
    ready(2)
    recv_table[...] = mul(w_recv[...], mid[...], TT).astype(BF16)
    wab = wa[...].astype(BF16)
    ready(3)
    for start in range(0, pre.shape[1], BLOCK):
        span = pl.ds(start, BLOCK)
        part = mul(recv_table[...], places(recv_table.shape[1], receiver[:, span]))
        pre[:, span] = (part + mul(wab, fa[:, span].astype(BF16), TN)).astype(pre.dtype)


def process_rest(
    mid, pre, listed, count_any, sender_any, receiver_any, out_any, in_any, node_any,
    result_any,
    count, sender, receiver, w_out, w_in, w_node, result, sems, out_sems,
):
    ready = fetch(
        (
            (sender_any, sender), (receiver_any, receiver), (count_any, count), (out_any, w_out),
            (in_any, w_in), (node_any, w_node),
        ),
        sems,
    )
    table = listed[...].T
    ready(0, 1, 2, 3)

    def to_of(i):
        return places(mid.shape[0], receiver[:, pl.ds(i * BLOCK, BLOCK)])

    def pre_of(i):
        span = pl.ds(i * BLOCK, BLOCK)
        return pre[:, span] + mul(table, places(table.shape[1], sender[:, span]))

    summed = summed_messages(sender.shape[1], pre_of, to_of, w_out, count[0])
    ready(4, 5)
    result[...] = nodes_of(mid[...], summed, w_in, w_node)
    fetch(((result, result_any),), out_sems)(0)


S, V, H = (pl.BlockSpec(memory_space=m) for m in (pltpu.SMEM, pltpu.VMEM, pltpu.HBM))
ONE = "one integer"


def shape(*sizes, dtype=BF16):
    return jax.ShapeDtypeStruct(sizes, dtype)


def call(kernel, name, near, far, near_outs, far_outs, scratch, copies):
    return pl.pallas_call(
        kernel,
        out_shape=near_outs + far_outs,
        in_specs=[V] * len(near) + [H] * len(far),
        out_specs=[V] * len(near_outs) + [H] * len(far_outs),
        scratch_shapes=[
            pltpu.SMEM((1,), jnp.int32) if s is ONE else pltpu.VMEM(s.shape, s.dtype)
            for s in scratch
        ]
        + [pltpu.SemaphoreType.DMA((n,)) for n in copies],
        compiler_params=pltpu.CompilerParams(vmem_limit_bytes=48 * 2**20),
        name=name,
    )(*near, *(x if x.size == 1 else pltpu.with_memory_space_constraint(x, pltpu.HBM) for x in far))


def body(
    grid_latent, mesh_latent, enc_feats, enc_sender, enc_receiver, enc_count,
    mesh_feats, mesh_sender, mesh_receiver, mesh_count, need_rows,
    w_enc_feat, w_enc_send, w_enc_recv, w_enc_out, w_enc_node_in, w_enc_node_out,
    w_proc_feat, w_proc_send, w_proc_recv, w_proc_out, w_proc_node_in, w_proc_node_out,
):
    nodes, width = mesh_latent.shape
    rows = grid_latent.shape[0]
    slots = enc_feats.shape[1]
    blocks = lax.axis_size("tile")
    per = need_rows.shape[2]
    square = shape(width, width)
    node_rows = shape(nodes, width)
    edge_index = shape(1, slots, dtype=jnp.int32)
    edge_feats = shape(*enc_feats.shape, dtype=F32)
    feat_weight = shape(*w_enc_feat.shape, dtype=F32)
    stacked = [shape(16, slots, dtype=F32), shape(16, width, dtype=F32)]
    enc_sender, enc_receiver, mesh_sender, mesh_receiver = (
        x.reshape(1, slots) for x in (enc_sender, enc_receiver, mesh_sender, mesh_receiver)
    )

    asked = lax.all_to_all(
        need_rows.reshape(blocks, 1, per), "tile", split_axis=0, concat_axis=0, tiled=True
    )
    for_pair, for_other = call(
        band_ends, "band_ends", [], [grid_latent], [], [shape(HALO, width)] * 2,
        [shape(HALO, width)] * 2, (2, 2),
    )
    pairs = [(i, i ^ 1) for i in range(blocks)]
    others = [(i, i + 1 if i % 2 else i - 1) for i in range(1, blocks - 1)]
    from_pair = lax.ppermute(for_pair, "tile", pairs)
    from_other = lax.ppermute(for_other, "tile", others)
    mid, sent = call(
        encode,
        "encode",
        [from_pair, from_other],
        [
            enc_count, enc_feats, enc_sender, enc_receiver, w_enc_feat, mesh_latent, w_enc_recv,
            w_enc_send, grid_latent, w_enc_out, w_enc_node_in, w_enc_node_out, w_proc_send,
        ],
        [node_rows, node_rows],
        [],
        [
            ONE, edge_feats, edge_index, edge_index, feat_weight, node_rows, square, square,
            shape(rows, width), square, shape(2 * width, width), square, square,
            shape(width, rows + 2 * HALO), shape(width, nodes),
        ]
        + stacked,
        (13,),
    )
    (outgoing,) = call(
        answer,
        "answer",
        [sent, asked],
        [],
        [],
        [shape(blocks * per, width)],
        [shape(blocks * per, width), shape(blocks, per, dtype=F32)],
        (1,),
    )
    listed = lax.all_to_all(
        outgoing.reshape(blocks, per, width), "tile", split_axis=0, concat_axis=0, tiled=True
    ).reshape(blocks * per, width)
    (pre,) = call(
        process_own,
        "process_own",
        [mid],
        [mesh_feats, mesh_receiver, w_proc_feat, w_proc_recv],
        [shape(width, slots)],
        [],
        [edge_feats, edge_index, feat_weight, square, shape(width, nodes)] + stacked,
        (4,),
    )
    (result,) = call(
        process_rest,
        "process_rest",
        [mid, pre, listed],
        [
            mesh_count, mesh_sender, mesh_receiver, w_proc_out, w_proc_node_in, w_proc_node_out,
        ],
        [],
        [node_rows],
        [
            ONE, edge_index, edge_index, square, shape(2 * width, width), square, node_rows,
        ],
        (6, 1),
    )
    return result


def solution(mesh):
    split_rows = P(("groups", "tile"), None)
    split_columns = P(None, ("groups", "tile"))
    split_flat = P(("groups", "tile"))
    placed = (
        split_rows, split_rows, split_columns, split_flat, split_flat, split_flat,
        split_columns, split_flat, split_flat, split_flat,
        P(("groups", "tile"), None, None),
    ) + (P(),) * 12
    return jax.shard_map(
        body, mesh=mesh, in_specs=placed, out_specs=split_rows, check_vma=False
    )
```

```python
import functools

import jax
import jax.numpy as jnp
from jax import lax
from jax.experimental import pallas as pl
from jax.experimental.pallas import tpu as pltpu
from jax.sharding import PartitionSpec as P

HALO = 256
BLOCK = 512
LANES = 128
F32, BF16 = jnp.float32, jnp.bfloat16
NN = (((1,), (0,)), ((), ()))
NT = (((1,), (1,)), ((), ()))
TN = (((0,), (0,)), ((), ()))
TT = (((0,), (1,)), ((), ()))


def mul(a, b, dims=NN):
    return lax.dot_general(a, b, dims, preferred_element_type=F32)


def swish_of_half(half):
    return half * jnp.tanh(half) + half


def norm(x, axis):
    size = x.shape[axis]
    centered = x - jnp.sum(x, axis=axis, keepdims=True) * (1.0 / size)
    variance = jnp.sum(centered * centered, axis=axis, keepdims=True) * (1.0 / size)
    return centered, lax.rsqrt(variance + 1e-05)


def places(rows, indices):
    at = lax.broadcasted_iota(jnp.int32, (rows, indices.shape[1]), 0).astype(jnp.int16)
    one, zero = jnp.array(1, BF16), jnp.array(0, BF16)
    return jnp.where(at == indices.astype(jnp.int16), one, zero)


def split(x):
    high = x.astype(BF16)
    return high, (x - high.astype(F32)).astype(BF16)


def stack_feats(feats, w_feat, fa, wa):
    rows = feats.shape[0]
    fa[...] = jnp.zeros(fa.shape, F32)
    wa[...] = jnp.zeros(wa.shape, F32)
    f_high, f_low = split(feats[...])
    w_high, w_low = split(0.5 * w_feat[...])
    for at, (f, w) in enumerate(((f_high, w_high), (f_high, w_low), (f_low, w_high))):
        fa[at * rows : (at + 1) * rows, :] = f.astype(F32)
        wa[at * rows : (at + 1) * rows, :] = w.astype(F32)


def fetch(pairs, sems):
    copies = [pltpu.make_async_copy(a, b, sems.at[i]) for i, (a, b) in enumerate(pairs)]
    for copy in copies:
        copy.start()

    def ready(*which):
        for i in which:
            copies[i].wait()

    return ready


def summed_messages(total, pre_of, to_of, w_out, count):
    w_out = w_out[...]
    held = {}

    def first(i):
        return to_of(i), swish_of_half(pre_of(i)).astype(BF16)

    def second(i, to, hidden):
        return to, mul(w_out, hidden, TN)

    def third(i, to, out):
        out, scale = norm(out, 0)
        live = lax.broadcasted_iota(jnp.int32, (1, BLOCK), 1) + i * BLOCK < count
        return to, (out * jnp.where(live, scale, 0.0)).astype(BF16)

    def last(i, to, message):
        return (mul(to, message, NT),)

    stages = (first, second, third, last)
    summed = None
    for step in range(total // BLOCK + len(stages) - 1):
        for at, stage in enumerate(stages):
            i = step - at
            if 0 <= i < total // BLOCK:
                held[i] = stage(i, *held.get(i, ()))
                if stage is last:
                    part = held.pop(i)[0]
                    summed = part if summed is None else summed + part
    return summed.astype(BF16)


def nodes_of(latent, first, summed, w_in, w_out):
    hidden = swish_of_half(0.5 * (first + mul(summed, w_in))).astype(BF16)
    centered, scale = norm(mul(hidden, w_out[...]), 1)
    return (latent.astype(F32) + centered * scale).astype(BF16)


def in_a_row(asked, rows):
    blocks, _, per = asked.shape
    for i in range(blocks):
        rows[i : i + 1, :] = asked[i].astype(F32)
    size = (per, blocks * per)
    column = lax.broadcasted_iota(jnp.int32, size, 1) % per
    repeat = (column == lax.broadcasted_iota(jnp.int32, size, 0)).astype(F32).astype(BF16)
    wide = mul(rows[...].astype(BF16), repeat)
    size = wide.shape
    block = lax.broadcasted_iota(jnp.int32, size, 1) // per
    own = block == lax.broadcasted_iota(jnp.int32, size, 0)
    return jnp.sum(jnp.where(own, wide, 0.0), axis=0, keepdims=True).astype(jnp.int32)


def band_ends(grid_any, grid, pair_any, other_any, sems, out_sems):
    first = (lax.axis_index("tile") % 2) * (grid.shape[0] - HALO)
    last = grid.shape[0] - HALO - first
    size = grid.shape[0] // sems.shape[0]
    spans = [pl.ds(i * size, size) for i in range(sems.shape[0])]
    fetch([(grid_any.at[span, :], grid.at[span, :]) for span in spans], sems)(*range(len(spans)))
    ends = [grid.at[pl.ds(pl.multiple_of(at, HALO), HALO), :] for at in (last, first)]
    fetch(((ends[0], pair_any), (ends[1], other_any)), out_sems)(0, 1)


def encode(
    from_pair, from_other, grid,
    count_any, feats_any, sender_any, receiver_any, feat_any, latent_any, recv_any, send_any,
    out_any, in_any, node_any, next_any,
    mid, sent,
    count, sender, feats, receiver, w_feat, latent, w_recv, w_send, w_out, w_in, w_node,
    w_next, first, table, picked, recv_table, fa, wa, sems,
):
    ready = fetch(
        (
            (sender_any, sender), (feats_any, feats), (feat_any, w_feat),
            (latent_any, latent), (recv_any, w_recv), (send_any, w_send),
            (receiver_any, receiver), (out_any, w_out), (count_any, count), (in_any, w_in),
            (node_any, w_node), (next_any, w_next),
        ),
        sems,
    )
    own, width = grid.shape
    parts = width // LANES
    odd = lax.axis_index("tile") % 2 == 1

    def place_rows(at, rows):
        for c in range(parts):
            span = pl.ds(at * parts + c, rows.shape[0], stride=parts)
            table[span, :] = rows[:, c * LANES : (c + 1) * LANES].astype(F32)

    place_rows(0, jnp.where(odd, from_pair[...], from_other[...]))
    place_rows(HALO + own, jnp.where(odd, from_other[...], from_pair[...]))
    place_rows(HALO, grid[...])
    ready(0)

    def gather(i):
        for e in range(i * BLOCK, (i + 1) * BLOCK):
            row = table[pl.ds(sender[0, e] * parts, parts), :]
            picked[pl.ds(e // 8 * (8 * parts) + e % 8, parts, stride=8), :] = row

    gather(0)
    ready(1, 2)
    stack_feats(feats, w_feat, fa, wa)
    ready(3, 4)
    recv_table[...] = (0.5 * mul(w_recv[...], latent[...], TT)).astype(BF16)
    wab = wa[...].astype(BF16)
    ready(5, 6, 7, 8)
    half_send = w_send[...] * jnp.array(0.5, BF16)

    def to_of(i):
        return places(recv_table.shape[1], receiver[:, pl.ds(i * BLOCK, BLOCK)])

    def pre_of(i):
        span = pl.ds(i * BLOCK, BLOCK)
        size = BLOCK * parts
        rows = picked[i * size : (i + 1) * size, :].reshape(BLOCK // 8, parts, 8, LANES)
        rows = [rows[:, c].reshape(BLOCK, LANES).astype(BF16) for c in range(parts)]
        pre = mul(half_send, jnp.concatenate(rows, axis=1), TT)
        if (i + 1) * BLOCK < picked.shape[0] // parts:
            gather(i + 1)
        pre += mul(recv_table[...], to_of(i))
        return pre + mul(wab, fa[:, span].astype(BF16), TN)

    ready(9)
    first[...] = mul(latent[...], w_in[:width, :])
    summed = summed_messages(receiver.shape[1], pre_of, to_of, w_out, count[0])
    ready(10, 11)
    middle = nodes_of(latent[...], first[...], summed, w_in[width:, :], w_node)
    mid[...] = middle
    sent[...] = (0.5 * mul(middle, w_next[...])).astype(BF16)


def answer(sent, asked, outgoing_any, outgoing, rows, sems):
    at = places(sent.shape[0], in_a_row(asked, rows))
    outgoing[...] = mul(at, sent[...], TN).astype(BF16)
    fetch(((outgoing, outgoing_any),), sems)(0)


def process_own(
    mid, feats_any, receiver_any, feat_any, recv_any, in_any, out_any, pre, w_out, first_any,
    feats, receiver, w_feat, w_recv, w_in, first, recv_table, fa, wa, sems, out_sems,
):
    ready = fetch(
        (
            (feats_any, feats), (feat_any, w_feat), (recv_any, w_recv), (receiver_any, receiver),
            (in_any.at[: w_in.shape[0], :], w_in), (out_any, w_out),
        ),
        sems,
    )
    ready(0, 1)
    stack_feats(feats, w_feat, fa, wa)
    ready(2)
    recv_table[...] = (0.5 * mul(w_recv[...], mid[...], TT)).astype(BF16)
    wab = wa[...].astype(BF16)
    ready(3)
    for start in range(0, pre.shape[1], BLOCK):
        span = pl.ds(start, BLOCK)
        part = mul(recv_table[...], places(recv_table.shape[1], receiver[:, span]))
        pre[:, span] = (part + mul(wab, fa[:, span].astype(BF16), TN)).astype(pre.dtype)
    ready(4)
    first[...] = mul(mid[...], w_in[...])
    fetch(((first, first_any),), out_sems)(0)
    ready(5)


def process_rest(
    mid, pre, listed, w_out, count_any, sender_any, receiver_any, first_any, in_any, node_any,
    result_any,
    count, sender, receiver, first, w_in, w_node, result, sems, out_sems,
):
    ready = fetch(
        (
            (sender_any, sender), (receiver_any, receiver), (count_any, count),
            (first_any, first), (in_any.at[w_in.shape[0] :, :], w_in), (node_any, w_node),
        ),
        sems,
    )
    table = listed[...].T
    ready(0, 1, 2)

    def to_of(i):
        return places(mid.shape[0], receiver[:, pl.ds(i * BLOCK, BLOCK)])

    def pre_of(i):
        span = pl.ds(i * BLOCK, BLOCK)
        return pre[:, span] + mul(table, places(table.shape[1], sender[:, span]))

    summed = summed_messages(sender.shape[1], pre_of, to_of, w_out, count[0])
    ready(3, 4, 5)
    result[...] = nodes_of(mid[...], first[...], summed, w_in[...], w_node)
    fetch(((result, result_any),), out_sems)(0)


S, V, H = (pl.BlockSpec(memory_space=m) for m in (pltpu.SMEM, pltpu.VMEM, pltpu.HBM))


class Scalars(jax.ShapeDtypeStruct):
    pass


def shape(*sizes, dtype=BF16):
    return jax.ShapeDtypeStruct(sizes, dtype)


def call(kernel, name, near, far, near_outs, far_outs, scratch, copies):
    return pl.pallas_call(
        kernel,
        out_shape=near_outs + far_outs,
        in_specs=[V] * len(near) + [H] * len(far),
        out_specs=[V] * len(near_outs) + [H] * len(far_outs),
        scratch_shapes=[
            (pltpu.SMEM if isinstance(s, Scalars) else pltpu.VMEM)(s.shape, s.dtype)
            for s in scratch
        ]
        + [pltpu.SemaphoreType.DMA((n,)) for n in copies],
        compiler_params=pltpu.CompilerParams(vmem_limit_bytes=48 * 2**20),
        name=name,
    )(*near, *(x if x.size == 1 else pltpu.with_memory_space_constraint(x, pltpu.HBM) for x in far))


def body(
    grid_latent, mesh_latent, enc_feats, enc_sender, enc_receiver, enc_count,
    mesh_feats, mesh_sender, mesh_receiver, mesh_count, need_rows,
    w_enc_feat, w_enc_send, w_enc_recv, w_enc_out, w_enc_node_in, w_enc_node_out,
    w_proc_feat, w_proc_send, w_proc_recv, w_proc_out, w_proc_node_in, w_proc_node_out,
):
    nodes, width = mesh_latent.shape
    rows = grid_latent.shape[0]
    slots = enc_feats.shape[1]
    blocks = lax.axis_size("tile")
    per = need_rows.shape[2]
    square = shape(width, width)
    one, scalars = (Scalars(n, jnp.int32) for n in ((1,), (1, slots)))
    node_rows = shape(nodes, width)
    edge_index = shape(1, slots, dtype=jnp.int32)
    edge_feats = shape(*enc_feats.shape, dtype=F32)
    feat_weight = shape(*w_enc_feat.shape, dtype=F32)
    stacked = [shape(16, slots, dtype=F32), shape(16, width, dtype=F32)]
    enc_sender, enc_receiver, mesh_sender, mesh_receiver = (
        x.reshape(1, slots) for x in (enc_sender, enc_receiver, mesh_sender, mesh_receiver)
    )

    asked = lax.all_to_all(
        need_rows.reshape(blocks, 1, per), "tile", split_axis=0, concat_axis=0, tiled=True
    )
    grid, for_pair, for_other = call(
        band_ends,
        "band_ends",
        [],
        [grid_latent],
        [shape(rows, width)],
        [shape(HALO, width)] * 2,
        [],
        (4, 2),
    )
    pairs = [(i, i ^ 1) for i in range(blocks)]
    others = [(i, i + 1 if i % 2 else i - 1) for i in range(1, blocks - 1)]
    from_pair = lax.ppermute(for_pair, "tile", pairs)
    from_other = lax.ppermute(for_other, "tile", others)
    mid, sent = call(
        encode,
        "encode",
        [from_pair, from_other, grid],
        [
            enc_count, enc_feats, enc_sender, enc_receiver, w_enc_feat, mesh_latent, w_enc_recv,
            w_enc_send, w_enc_out, w_enc_node_in, w_enc_node_out, w_proc_send,
        ],
        [node_rows, node_rows],
        [],
        [
            one, scalars, edge_feats, edge_index, feat_weight, node_rows, square, square,
            square, shape(2 * width, width), square, square, shape(nodes, width, dtype=F32),
            shape((rows + 2 * HALO) * width // LANES, LANES, dtype=F32),
            shape(slots * width // LANES, LANES, dtype=F32), shape(width, nodes),
        ]
        + stacked,
        (12,),
    )
    (outgoing,) = call(
        answer,
        "answer",
        [sent, asked],
        [],
        [],
        [shape(blocks * per, width)],
        [shape(blocks * per, width), shape(blocks, per, dtype=F32)],
        (1,),
    )
    listed = lax.all_to_all(
        outgoing.reshape(blocks, per, width), "tile", split_axis=0, concat_axis=0, tiled=True
    ).reshape(blocks * per, width)
    pre, w_out, first = call(
        process_own,
        "process_own",
        [mid],
        [mesh_feats, mesh_receiver, w_proc_feat, w_proc_recv, w_proc_node_in, w_proc_out],
        [shape(width, slots), square],
        [shape(nodes, width, dtype=F32)],
        [
            edge_feats, edge_index, feat_weight, square, square,
            shape(nodes, width, dtype=F32), shape(width, nodes),
        ]
        + stacked,
        (6, 1),
    )
    (result,) = call(
        process_rest,
        "process_rest",
        [mid, pre, listed, w_out],
        [mesh_count, mesh_sender, mesh_receiver, first, w_proc_node_in, w_proc_node_out],
        [],
        [node_rows],
        [
            one, edge_index, edge_index, shape(nodes, width, dtype=F32), square, square,
            node_rows,
        ],
        (6, 1),
    )
    return result


def solution(mesh):
    split_rows = P(("groups", "tile"), None)
    split_columns = P(None, ("groups", "tile"))
    split_flat = P(("groups", "tile"))
    placed = (
        split_rows, split_rows, split_columns, split_flat, split_flat, split_flat,
        split_columns, split_flat, split_flat, split_flat,
        P(("groups", "tile"), None, None),
    ) + (P(),) * 12
    return jax.shard_map(
        body, mesh=mesh, in_specs=placed, out_specs=split_rows, check_vma=False
    )
```

```python
import functools

import jax
import jax.numpy as jnp
from jax import lax
from jax.experimental import pallas as pl
from jax.experimental.pallas import tpu as pltpu
from jax.sharding import PartitionSpec as P

HALO = 256
BLOCK = 512
LANES = 128
SPARE = 64
F32, BF16 = jnp.float32, jnp.bfloat16
NN = (((1,), (0,)), ((), ()))
NT = (((1,), (1,)), ((), ()))
TN = (((0,), (0,)), ((), ()))
TT = (((0,), (1,)), ((), ()))


def mul(a, b, dims=NN):
    return lax.dot_general(a, b, dims, preferred_element_type=F32)


def swish_of_half(half):
    return half * jnp.tanh(half) + half


def norm(x, axis):
    size = x.shape[axis]
    centered = x - jnp.sum(x, axis=axis, keepdims=True) * (1.0 / size)
    variance = jnp.sum(centered * centered, axis=axis, keepdims=True) * (1.0 / size)
    return centered, lax.rsqrt(variance + 1e-05)


def places(rows, indices):
    at = lax.broadcasted_iota(jnp.int32, (rows, indices.shape[1]), 0).astype(jnp.int16)
    one, zero = jnp.array(1, BF16), jnp.array(0, BF16)
    return jnp.where(at == indices.astype(jnp.int16), one, zero)


def split(x):
    high = x.astype(BF16)
    return high, (x - high.astype(F32)).astype(BF16)


def stack_feats(feats, w_feat, fa, wa):
    rows = feats.shape[0]
    fa[...] = jnp.zeros(fa.shape, F32)
    wa[...] = jnp.zeros(wa.shape, F32)
    f_high, f_low = split(feats[...])
    w_high, w_low = split(0.5 * w_feat[...])
    for at, (f, w) in enumerate(((f_high, w_high), (f_high, w_low), (f_low, w_high))):
        fa[at * rows : (at + 1) * rows, :] = f.astype(F32)
        wa[at * rows : (at + 1) * rows, :] = w.astype(F32)


def fetch(pairs, sems):
    copies = [pltpu.make_async_copy(a, b, sems.at[i]) for i, (a, b) in enumerate(pairs)]
    for copy in copies:
        copy.start()

    def ready(*which):
        for i in which:
            copies[i].wait()

    return ready


def summed_messages(total, pre_of, to_of, w_out, count):
    w_out = w_out[...]
    held = {}

    def first(i):
        return to_of(i), swish_of_half(pre_of(i)).astype(BF16)

    def second(i, to, hidden):
        return to, mul(w_out, hidden, TN)

    def third(i, to, out):
        one, part = out[:1, :], 1.0 / out.shape[0]
        moved = out - one
        mean = jnp.sum(moved, axis=0, keepdims=True) * part
        variance = jnp.sum(moved * moved, axis=0, keepdims=True) * part - mean * mean
        scale = lax.rsqrt(jnp.maximum(variance, 0.0) + 1e-05)
        live = lax.broadcasted_iota(jnp.int32, (1, BLOCK), 1) + i * BLOCK < count
        return to, ((out - (mean + one)) * jnp.where(live, scale, 0.0)).astype(BF16)

    def last(i, to, message):
        return (mul(to, message, NT),)

    stages = (first, second, third, last)
    summed = None
    for step in range(total // BLOCK + len(stages) - 1):
        for at, stage in enumerate(stages):
            i = step - at
            if 0 <= i < total // BLOCK:
                held[i] = stage(i, *held.get(i, ()))
                if stage is last:
                    part = held.pop(i)[0]
                    summed = part if summed is None else summed + part
    return summed.astype(BF16)


def nodes_of(latent, first, summed, w_in, w_out):
    hidden = swish_of_half(0.5 * (first + mul(summed, w_in))).astype(BF16)
    centered, scale = norm(mul(hidden, w_out[...]), 1)
    return (latent.astype(F32) + centered * scale).astype(BF16)


def in_a_column(asked):
    blocks, _, per = asked.shape
    size = (blocks, per, per)
    own = lax.broadcasted_iota(jnp.int32, size, 1) == lax.broadcasted_iota(jnp.int32, size, 2)
    column = jnp.sum(jnp.where(own, asked.astype(F32), 0.0), axis=2, keepdims=True)
    return column.reshape(blocks * per, 1).astype(jnp.int32)


def band_ends(
    grid_any, latent_any, feats_any, receiver_any,
    pair, other, middle, latent, feats, receiver, sems,
):
    last = grid_any.shape[0] - HALO
    first = (lax.axis_index("tile") % 2) * last
    pair_at, other_at = (pl.ds(pl.multiple_of(at, HALO), HALO) for at in (last - first, first))
    fetch(
        (
            (grid_any.at[pair_at, :], pair), (grid_any.at[other_at, :], other),
            (grid_any.at[HALO:last, :], middle), (latent_any, latent), (feats_any, feats),
            (receiver_any, receiver),
        ),
        sems,
    )(*range(6))


def encode(
    from_pair, from_other, pair, other, middle, latent, feats, receiver,
    count_any, sender_any, feat_any, recv_any, send_any, out_any, in_any, node_any, next_any,
    mid, sent,
    count, sender, w_feat, w_recv, w_send, w_out, w_in, w_node, w_next,
    first, table, picked, recv_table, fa, wa, sems,
):
    ready = fetch(
        (
            (sender_any, sender), (feat_any, w_feat), (recv_any, w_recv), (send_any, w_send),
            (out_any, w_out), (count_any, count), (in_any, w_in), (node_any, w_node),
            (next_any, w_next),
        ),
        sems,
    )
    own, width = middle.shape[0] + 2 * HALO, middle.shape[1]
    parts = width // LANES
    odd = lax.axis_index("tile") % 2 == 1

    def place_rows(at, rows):
        for c in range(parts):
            span = pl.ds(at * parts + c, rows.shape[0], stride=parts)
            table[span, :] = rows[:, c * LANES : (c + 1) * LANES].astype(F32)

    place_rows(2 * HALO, middle[...])
    place_rows(HALO, jnp.where(odd, pair[...], other[...]))
    place_rows(own, jnp.where(odd, other[...], pair[...]))
    place_rows(0, jnp.where(odd, from_pair[...], from_other[...]))
    place_rows(HALO + own, jnp.where(odd, from_other[...], from_pair[...]))
    ready(0, 1)

    def gather(i):
        for e in range(i * BLOCK, (i + 1) * BLOCK):
            row = table[pl.ds(sender[0, e] * parts, parts), :]
            picked[pl.ds(e // 8 * (8 * parts) + e % 8, parts, stride=8), :] = row

    gather(0)
    stack_feats(feats, w_feat, fa, wa)
    ready(2)
    recv_table[...] = (0.5 * mul(w_recv[...], latent[...], TT)).astype(BF16)
    wab = wa[...].astype(BF16)
    ready(3, 4, 5)
    half_send = w_send[...] * jnp.array(0.5, BF16)

    def to_of(i):
        return places(recv_table.shape[1], receiver[:, pl.ds(i * BLOCK, BLOCK)])

    def pre_of(i):
        span = pl.ds(i * BLOCK, BLOCK)
        size = BLOCK * parts
        rows = picked[i * size : (i + 1) * size, :].reshape(BLOCK // 8, parts, 8, LANES)
        rows = [rows[:, c].reshape(BLOCK, LANES).astype(BF16) for c in range(parts)]
        pre = mul(half_send, jnp.concatenate(rows, axis=1), TT)
        if (i + 1) * BLOCK < receiver.shape[1]:
            gather(i + 1)
        pre += mul(recv_table[...], to_of(i))
        return pre + mul(wab, fa[:, span].astype(BF16), TN)

    ready(6)
    first[...] = mul(latent[...], w_in[:width, :])
    summed = summed_messages(receiver.shape[1], pre_of, to_of, w_out, count[0])
    ready(7, 8)
    middle = nodes_of(latent[...], first[...], summed, w_in[width:, :], w_node)
    mid[...] = middle
    sent[...] = (0.5 * mul(middle, w_next[...])).astype(BF16)


def answer(sent, asked, outgoing_any, outgoing, sems):
    column = in_a_column(asked[...])
    size = (column.shape[0], sent.shape[0])
    at = (lax.broadcasted_iota(jnp.int32, size, 1) == column).astype(F32).astype(BF16)
    part = size[0] // sems.shape[0]
    copies = []
    for i in range(sems.shape[0]):
        span = pl.ds(i * part, part)
        outgoing[span, :] = mul(at[i * part : (i + 1) * part, :], sent[...]).astype(BF16)
        copies.append(
            pltpu.make_async_copy(outgoing.at[span, :], outgoing_any.at[span, :], sems.at[i])
        )
        copies[-1].start()
    for copy in copies:
        copy.wait()


def process_own(
    mid, feats_any, receiver_any, feat_any, recv_any, in_any, out_any, pre, w_out, first_any,
    feats, receiver, w_feat, w_recv, w_in, first, recv_table, fa, wa, sems, out_sems,
):
    ready = fetch(
        (
            (feats_any, feats), (feat_any, w_feat), (recv_any, w_recv), (receiver_any, receiver),
            (in_any.at[: w_in.shape[0], :], w_in), (out_any, w_out),
        ),
        sems,
    )
    ready(0, 1)
    stack_feats(feats, w_feat, fa, wa)
    ready(2)
    recv_table[...] = (0.5 * mul(w_recv[...], mid[...], TT)).astype(BF16)
    wab = wa[...].astype(BF16)
    ready(3)
    for start in range(0, pre.shape[1], BLOCK):
        span = pl.ds(start, BLOCK)
        part = mul(recv_table[...], places(recv_table.shape[1], receiver[:, span]))
        pre[:, span] = (part + mul(wab, fa[:, span].astype(BF16), TN)).astype(pre.dtype)
    ready(4)
    first[...] = mul(mid[...], w_in[...])
    fetch(((first, first_any),), out_sems)(0)
    ready(5)


def process_rest(
    mid, pre, listed, w_out, count_any, sender_any, receiver_any, first_any, in_any, node_any,
    result_any,
    count, sender, receiver, first, w_in, w_node, result, sems, out_sems,
):
    ready = fetch(
        (
            (sender_any, sender), (receiver_any, receiver), (count_any, count),
            (first_any, first), (in_any.at[w_in.shape[0] :, :], w_in), (node_any, w_node),
        ),
        sems,
    )
    table = listed[...].T
    ready(0, 1, 2)

    def to_of(i):
        return places(mid.shape[0], receiver[:, pl.ds(i * BLOCK, BLOCK)])

    def pre_of(i):
        span = pl.ds(i * BLOCK, BLOCK)
        return pre[:, span] + mul(table, places(table.shape[1], sender[:, span]))

    summed = summed_messages(sender.shape[1], pre_of, to_of, w_out, count[0])
    ready(3, 4, 5)
    result[...] = nodes_of(mid[...], first[...], summed, w_in[...], w_node)
    fetch(((result, result_any),), out_sems)(0)


S, V, H = (pl.BlockSpec(memory_space=m) for m in (pltpu.SMEM, pltpu.VMEM, pltpu.HBM))


class Scalars(jax.ShapeDtypeStruct):
    pass


def shape(*sizes, dtype=BF16):
    return jax.ShapeDtypeStruct(sizes, dtype)


def call(kernel, name, near, far, near_outs, far_outs, scratch, copies):
    return pl.pallas_call(
        kernel,
        out_shape=near_outs + far_outs,
        in_specs=[V] * len(near) + [H] * len(far),
        out_specs=[V] * len(near_outs) + [H] * len(far_outs),
        scratch_shapes=[
            (pltpu.SMEM if isinstance(s, Scalars) else pltpu.VMEM)(s.shape, s.dtype)
            for s in scratch
        ]
        + [pltpu.SemaphoreType.DMA((n,)) for n in copies],
        compiler_params=pltpu.CompilerParams(vmem_limit_bytes=48 * 2**20),
        name=name,
    )(*near, *(x if x.size == 1 else pltpu.with_memory_space_constraint(x, pltpu.HBM) for x in far))


def body(
    grid_latent, mesh_latent, enc_feats, enc_sender, enc_receiver, enc_count,
    mesh_feats, mesh_sender, mesh_receiver, mesh_count, need_rows,
    w_enc_feat, w_enc_send, w_enc_recv, w_enc_out, w_enc_node_in, w_enc_node_out,
    w_proc_feat, w_proc_send, w_proc_recv, w_proc_out, w_proc_node_in, w_proc_node_out,
):
    nodes, width = mesh_latent.shape
    rows = grid_latent.shape[0]
    slots = enc_feats.shape[1]
    blocks = lax.axis_size("tile")
    per = need_rows.shape[2]
    square = shape(width, width)
    one, scalars = (Scalars(n, jnp.int32) for n in ((1,), (1, slots)))
    node_rows = shape(nodes, width)
    edge_index = shape(1, slots, dtype=jnp.int32)
    edge_feats = shape(*enc_feats.shape, dtype=F32)
    feat_weight = shape(*w_enc_feat.shape, dtype=F32)
    stacked = [shape(16, slots, dtype=F32), shape(16, width, dtype=F32)]
    enc_sender, enc_receiver, mesh_sender, mesh_receiver = (
        x.reshape(1, slots) for x in (enc_sender, enc_receiver, mesh_sender, mesh_receiver)
    )

    asked = lax.all_to_all(
        need_rows.reshape(blocks, 1, per), "tile", split_axis=0, concat_axis=0, tiled=True
    )
    near = call(
        band_ends,
        "band_ends",
        [],
        [grid_latent, mesh_latent, enc_feats, enc_receiver],
        [
            shape(HALO, width), shape(HALO, width), shape(rows - 2 * HALO, width), node_rows,
            edge_feats, edge_index,
        ],
        [],
        [],
        (6,),
    )
    for_pair, for_other = near[:2]
    pairs = [(i, i ^ 1) for i in range(blocks)]
    others = [(i, i + 1 if i % 2 else i - 1) for i in range(1, blocks - 1)]
    from_pair = lax.ppermute(for_pair, "tile", pairs)
    from_other = lax.ppermute(for_other, "tile", others)
    mid, sent = call(
        encode,
        "encode",
        [from_pair, from_other, *near],
        [
            enc_count, enc_sender, w_enc_feat, w_enc_recv, w_enc_send, w_enc_out, w_enc_node_in,
            w_enc_node_out, w_proc_send,
        ],
        [node_rows, node_rows],
        [],
        [
            one, scalars, feat_weight, square, square, square, shape(2 * width, width), square,
            square,
            shape(nodes, width, dtype=F32),
            shape((rows + 2 * HALO) * width // LANES + SPARE, LANES, dtype=F32),
            shape(slots * width // LANES + SPARE, LANES, dtype=F32), shape(width, nodes),
        ]
        + stacked,
        (9,),
    )
    (outgoing,) = call(
        answer,
        "answer",
        [sent, asked],
        [],
        [],
        [shape(blocks * per, width)],
        [shape(blocks * per, width)],
        (2,),
    )
    listed = lax.all_to_all(
        outgoing.reshape(blocks, per, width), "tile", split_axis=0, concat_axis=0, tiled=True
    ).reshape(blocks * per, width)
    pre, w_out, first = call(
        process_own,
        "process_own",
        [mid],
        [mesh_feats, mesh_receiver, w_proc_feat, w_proc_recv, w_proc_node_in, w_proc_out],
        [shape(width, slots), square],
        [shape(nodes, width, dtype=F32)],
        [
            edge_feats, edge_index, feat_weight, square, square,
            shape(nodes, width, dtype=F32), shape(width, nodes),
        ]
        + stacked,
        (6, 1),
    )
    (result,) = call(
        process_rest,
        "process_rest",
        [mid, pre, listed, w_out],
        [mesh_count, mesh_sender, mesh_receiver, first, w_proc_node_in, w_proc_node_out],
        [],
        [node_rows],
        [
            one, edge_index, edge_index, shape(nodes, width, dtype=F32), square, square,
            node_rows,
        ],
        (6, 1),
    )
    return result


def solution(mesh):
    split_rows = P(("groups", "tile"), None)
    split_columns = P(None, ("groups", "tile"))
    split_flat = P(("groups", "tile"))
    placed = (
        split_rows, split_rows, split_columns, split_flat, split_flat, split_flat,
        split_columns, split_flat, split_flat, split_flat,
        P(("groups", "tile"), None, None),
    ) + (P(),) * 12
    return jax.shard_map(
        body, mesh=mesh, in_specs=placed, out_specs=split_rows, check_vma=False
    )
```

```python
import functools

import jax
import jax.numpy as jnp
from jax import lax
from jax.experimental import pallas as pl
from jax.experimental.pallas import tpu as pltpu
from jax.sharding import PartitionSpec as P

HALO = 256
BLOCK = 512
LANES = 128
SPARE = 64
F32, BF16 = jnp.float32, jnp.bfloat16
NN = (((1,), (0,)), ((), ()))
NT = (((1,), (1,)), ((), ()))
TN = (((0,), (0,)), ((), ()))
TT = (((0,), (1,)), ((), ()))


def mul(a, b, dims=NN):
    return lax.dot_general(a, b, dims, preferred_element_type=F32)


def swish_of_half(half):
    return half * jnp.tanh(half) + half


def norm(x, axis):
    size = x.shape[axis]
    centered = x - jnp.sum(x, axis=axis, keepdims=True) * (1.0 / size)
    variance = jnp.sum(centered * centered, axis=axis, keepdims=True) * (1.0 / size)
    return centered, lax.rsqrt(variance + 1e-05)


def places(rows, indices):
    at = lax.broadcasted_iota(jnp.int32, (rows, indices.shape[1]), 0).astype(jnp.int16)
    one, zero = jnp.array(1, BF16), jnp.array(0, BF16)
    return jnp.where(at == indices.astype(jnp.int16), one, zero)


def split(x):
    high = x.astype(BF16)
    return high, (x - high.astype(F32)).astype(BF16)


def stack_feats(feats, w_feat, fa, wa):
    rows = feats.shape[0]
    fa[...] = jnp.zeros(fa.shape, F32)
    wa[...] = jnp.zeros(wa.shape, F32)
    f_high, f_low = split(feats[...])
    w_high, w_low = split(0.5 * w_feat[...])
    for at, (f, w) in enumerate(((f_high, w_high), (f_high, w_low), (f_low, w_high))):
        fa[at * rows : (at + 1) * rows, :] = f.astype(F32)
        wa[at * rows : (at + 1) * rows, :] = w.astype(F32)


def fetch(pairs, sems):
    copies = [pltpu.make_async_copy(a, b, sems.at[i]) for i, (a, b) in enumerate(pairs)]
    for copy in copies:
        copy.start()

    def ready(*which):
        for i in which:
            copies[i].wait()

    return ready


def summed_messages(total, pre_of, to_of, w_out, count):
    w_out = w_out[...]
    held = {}

    def first(i):
        return to_of(i), swish_of_half(pre_of(i)).astype(BF16)

    def second(i, to, hidden):
        return to, mul(w_out, hidden, TN)

    def third(i, to, out):
        one, part = out[:1, :], 1.0 / out.shape[0]
        moved = out - one
        mean = jnp.sum(moved, axis=0, keepdims=True) * part
        variance = jnp.sum(moved * moved, axis=0, keepdims=True) * part - mean * mean
        scale = lax.rsqrt(jnp.maximum(variance, 0.0) + 1e-05)
        live = lax.broadcasted_iota(jnp.int32, (1, BLOCK), 1) + i * BLOCK < count
        return to, ((out - (mean + one)) * jnp.where(live, scale, 0.0)).astype(BF16)

    def last(i, to, message):
        return (mul(to, message, NT),)

    stages = (first, second, third, last)
    summed = None
    for step in range(total // BLOCK + len(stages) - 1):
        for at, stage in enumerate(stages):
            i = step - at
            if 0 <= i < total // BLOCK:
                held[i] = stage(i, *held.get(i, ()))
                if stage is last:
                    part = held.pop(i)[0]
                    summed = part if summed is None else summed + part
    return summed.astype(BF16)


def nodes_of(latent, first, summed, w_in, w_out):
    hidden = swish_of_half(0.5 * (first + mul(summed, w_in))).astype(BF16)
    centered, scale = norm(mul(hidden, w_out[...]), 1)
    return (latent.astype(F32) + centered * scale).astype(BF16)


def in_a_column(asked):
    blocks, _, per = asked.shape
    size = (blocks, per, per)
    own = lax.broadcasted_iota(jnp.int32, size, 1) == lax.broadcasted_iota(jnp.int32, size, 2)
    column = jnp.sum(jnp.where(own, asked.astype(F32), 0.0), axis=2, keepdims=True)
    return column.reshape(blocks * per, 1).astype(jnp.int32)


def band_ends(
    grid_any, latent_any, feats_any, receiver_any,
    pair, other, middle, latent, feats, receiver, sems,
):
    last = grid_any.shape[0] - HALO
    first = (lax.axis_index("tile") % 2) * last
    pair_at, other_at = (pl.ds(pl.multiple_of(at, HALO), HALO) for at in (last - first, first))
    fetch(
        (
            (grid_any.at[pair_at, :], pair), (grid_any.at[other_at, :], other),
            (grid_any.at[HALO:last, :], middle), (latent_any, latent), (feats_any, feats),
            (receiver_any, receiver),
        ),
        sems,
    )(*range(6))


def encode(
    from_pair, from_other, pair, other, middle, latent, feats, receiver,
    count_any, sender_any, feat_any, recv_any, send_any, out_any, in_any, node_any, next_any,
    mid, sent,
    count, sender, w_feat, w_recv, w_send, w_out, w_in, w_node, w_next,
    first, table, picked, recv_table, fa, wa, sems,
):
    ready = fetch(
        (
            (sender_any, sender), (feat_any, w_feat), (recv_any, w_recv), (send_any, w_send),
            (out_any, w_out), (count_any, count), (in_any, w_in), (node_any, w_node),
            (next_any, w_next),
        ),
        sems,
    )
    own, width = middle.shape[0] + 2 * HALO, middle.shape[1]
    parts = width // LANES
    odd = lax.axis_index("tile") % 2 == 1

    def place_rows(at, rows):
        for c in range(parts):
            span = pl.ds(at * parts + c, rows.shape[0], stride=parts)
            table[span, :] = rows[:, c * LANES : (c + 1) * LANES].astype(F32)

    place_rows(2 * HALO, middle[...])
    place_rows(HALO, jnp.where(odd, pair[...], other[...]))
    place_rows(own, jnp.where(odd, other[...], pair[...]))
    place_rows(0, jnp.where(odd, from_pair[...], from_other[...]))
    place_rows(HALO + own, jnp.where(odd, from_other[...], from_pair[...]))
    ready(0, 1)

    def gather(i):
        for e in range(i * BLOCK, (i + 1) * BLOCK):
            row = table[pl.ds(sender[0, e] * parts, parts), :]
            picked[pl.ds(e // 8 * (8 * parts) + e % 8, parts, stride=8), :] = row

    gather(0)
    stack_feats(feats, w_feat, fa, wa)
    ready(2)
    recv_table[...] = (0.5 * mul(w_recv[...], latent[...], TT)).astype(BF16)
    wab = wa[...].astype(BF16)
    ready(3, 4, 5)
    half_send = w_send[...] * jnp.array(0.5, BF16)

    def to_of(i):
        return places(recv_table.shape[1], receiver[:, pl.ds(i * BLOCK, BLOCK)])

    def pre_of(i):
        span = pl.ds(i * BLOCK, BLOCK)
        size = BLOCK * parts
        rows = picked[i * size : (i + 1) * size, :].reshape(BLOCK // 8, parts, 8, LANES)
        rows = [rows[:, c].reshape(BLOCK, LANES).astype(BF16) for c in range(parts)]
        pre = mul(half_send, jnp.concatenate(rows, axis=1), TT)
        if (i + 1) * BLOCK < receiver.shape[1]:
            gather(i + 1)
        pre += mul(recv_table[...], to_of(i))
        return pre + mul(wab, fa[:, span].astype(BF16), TN)

    ready(6)
    first[...] = mul(latent[...], w_in[:width, :])
    summed = summed_messages(receiver.shape[1], pre_of, to_of, w_out, count[0])
    ready(7, 8)
    middle = nodes_of(latent[...], first[...], summed, w_in[width:, :], w_node)
    mid[...] = middle
    sent[...] = (0.5 * mul(middle, w_next[...])).astype(BF16)


def answer(sent, asked, outgoing_any, outgoing, sems):
    column = in_a_column(asked[...])
    size = (column.shape[0], sent.shape[0])
    at = (lax.broadcasted_iota(jnp.int32, size, 1) == column).astype(F32).astype(BF16)
    part = size[0] // sems.shape[0]
    copies = []
    for i in range(sems.shape[0]):
        span = pl.ds(i * part, part)
        outgoing[span, :] = mul(at[i * part : (i + 1) * part, :], sent[...]).astype(BF16)
        copies.append(
            pltpu.make_async_copy(outgoing.at[span, :], outgoing_any.at[span, :], sems.at[i])
        )
        copies[-1].start()
    for copy in copies:
        copy.wait()


def process_own(
    mid, feats_any, sender_any, receiver_any, feat_any, recv_any, in_any, out_any,
    pre, sender, receiver, w_out, first_any,
    feats, w_feat, w_recv, w_in, first, recv_table, fa, wa, sems, out_sems,
):
    ready = fetch(
        (
            (feats_any, feats), (feat_any, w_feat), (recv_any, w_recv), (receiver_any, receiver),
            (in_any.at[: w_in.shape[0], :], w_in), (out_any, w_out), (sender_any, sender),
        ),
        sems,
    )
    ready(0, 1)
    stack_feats(feats, w_feat, fa, wa)
    ready(2)
    recv_table[...] = (0.5 * mul(w_recv[...], mid[...], TT)).astype(BF16)
    wab = wa[...].astype(BF16)
    ready(3)
    for start in range(0, pre.shape[1], BLOCK):
        span = pl.ds(start, BLOCK)
        part = mul(recv_table[...], places(recv_table.shape[1], receiver[:, span]))
        pre[:, span] = (part + mul(wab, fa[:, span].astype(BF16), TN)).astype(pre.dtype)
    ready(4)
    first[...] = mul(mid[...], w_in[...])
    fetch(((first, first_any),), out_sems)(0)
    ready(5, 6)


def process_rest(
    mid, pre, sender, receiver, listed, w_out, count_any, first_any, in_any, node_any,
    result_any,
    count, first, w_in, w_node, result, sems, out_sems,
):
    ready = fetch(
        (
            (count_any, count), (first_any, first), (in_any.at[w_in.shape[0] :, :], w_in), (node_any, w_node),
        ),
        sems,
    )
    table = listed[...].T

    def to_of(i):
        return places(mid.shape[0], receiver[:, pl.ds(i * BLOCK, BLOCK)])

    def pre_of(i):
        span = pl.ds(i * BLOCK, BLOCK)
        return pre[:, span] + mul(table, places(table.shape[1], sender[:, span]))

    ready(0)
    summed = summed_messages(sender.shape[1], pre_of, to_of, w_out, count[0])
    ready(1, 2, 3)
    result[...] = nodes_of(mid[...], first[...], summed, w_in[...], w_node)
    fetch(((result, result_any),), out_sems)(0)


S, V, H = (pl.BlockSpec(memory_space=m) for m in (pltpu.SMEM, pltpu.VMEM, pltpu.HBM))


class Scalars(jax.ShapeDtypeStruct):
    pass


def shape(*sizes, dtype=BF16):
    return jax.ShapeDtypeStruct(sizes, dtype)


def call(kernel, name, near, far, near_outs, far_outs, scratch, copies):
    return pl.pallas_call(
        kernel,
        out_shape=near_outs + far_outs,
        in_specs=[V] * len(near) + [H] * len(far),
        out_specs=[V] * len(near_outs) + [H] * len(far_outs),
        scratch_shapes=[
            (pltpu.SMEM if isinstance(s, Scalars) else pltpu.VMEM)(s.shape, s.dtype)
            for s in scratch
        ]
        + [pltpu.SemaphoreType.DMA((n,)) for n in copies],
        compiler_params=pltpu.CompilerParams(vmem_limit_bytes=48 * 2**20),
        name=name,
    )(*near, *(x if x.size == 1 else pltpu.with_memory_space_constraint(x, pltpu.HBM) for x in far))


def body(
    grid_latent, mesh_latent, enc_feats, enc_sender, enc_receiver, enc_count,
    mesh_feats, mesh_sender, mesh_receiver, mesh_count, need_rows,
    w_enc_feat, w_enc_send, w_enc_recv, w_enc_out, w_enc_node_in, w_enc_node_out,
    w_proc_feat, w_proc_send, w_proc_recv, w_proc_out, w_proc_node_in, w_proc_node_out,
):
    nodes, width = mesh_latent.shape
    rows = grid_latent.shape[0]
    slots = enc_feats.shape[1]
    blocks = lax.axis_size("tile")
    per = need_rows.shape[2]
    square = shape(width, width)
    one, scalars = (Scalars(n, jnp.int32) for n in ((1,), (1, slots)))
    node_rows = shape(nodes, width)
    edge_index = shape(1, slots, dtype=jnp.int32)
    edge_feats = shape(*enc_feats.shape, dtype=F32)
    feat_weight = shape(*w_enc_feat.shape, dtype=F32)
    stacked = [shape(16, slots, dtype=F32), shape(16, width, dtype=F32)]
    enc_sender, enc_receiver, mesh_sender, mesh_receiver = (
        x.reshape(1, slots) for x in (enc_sender, enc_receiver, mesh_sender, mesh_receiver)
    )

    asked = lax.all_to_all(
        need_rows.reshape(blocks, 1, per), "tile", split_axis=0, concat_axis=0, tiled=True
    )
    near = call(
        band_ends,
        "band_ends",
        [],
        [grid_latent, mesh_latent, enc_feats, enc_receiver],
        [
            shape(HALO, width), shape(HALO, width), shape(rows - 2 * HALO, width), node_rows,
            edge_feats, edge_index,
        ],
        [],
        [],
        (6,),
    )
    for_pair, for_other = near[:2]
    pairs = [(i, i ^ 1) for i in range(blocks)]
    others = [(i, i + 1 if i % 2 else i - 1) for i in range(1, blocks - 1)]
    from_pair = lax.ppermute(for_pair, "tile", pairs)
    from_other = lax.ppermute(for_other, "tile", others)
    mid, sent = call(
        encode,
        "encode",
        [from_pair, from_other, *near],
        [
            enc_count, enc_sender, w_enc_feat, w_enc_recv, w_enc_send, w_enc_out, w_enc_node_in,
            w_enc_node_out, w_proc_send,
        ],
        [node_rows, node_rows],
        [],
        [
            one, scalars, feat_weight, square, square, square, shape(2 * width, width), square,
            square,
            shape(nodes, width, dtype=F32),
            shape((rows + 2 * HALO) * width // LANES + SPARE, LANES, dtype=F32),
            shape(slots * width // LANES + SPARE, LANES, dtype=F32), shape(width, nodes),
        ]
        + stacked,
        (9,),
    )
    (outgoing,) = call(
        answer,
        "answer",
        [sent, asked],
        [],
        [],
        [shape(blocks * per, width)],
        [shape(blocks * per, width)],
        (2,),
    )
    listed = lax.all_to_all(
        outgoing.reshape(blocks, per, width), "tile", split_axis=0, concat_axis=0, tiled=True
    ).reshape(blocks * per, width)
    pre, near_sender, near_receiver, w_out, first = call(
        process_own,
        "process_own",
        [mid],
        [
            mesh_feats, mesh_sender, mesh_receiver, w_proc_feat, w_proc_recv, w_proc_node_in,
            w_proc_out,
        ],
        [shape(width, slots), edge_index, edge_index, square],
        [shape(nodes, width, dtype=F32)],
        [
            edge_feats, feat_weight, square, square, shape(nodes, width, dtype=F32),
            shape(width, nodes),
        ]
        + stacked,
        (7, 1),
    )
    (result,) = call(
        process_rest,
        "process_rest",
        [mid, pre, near_sender, near_receiver, listed, w_out],
        [mesh_count, first, w_proc_node_in, w_proc_node_out],
        [],
        [node_rows],
        [
            one, shape(nodes, width, dtype=F32), square, square, node_rows,
        ],
        (4, 1),
    )
    return result


def solution(mesh):
    split_rows = P(("groups", "tile"), None)
    split_columns = P(None, ("groups", "tile"))
    split_flat = P(("groups", "tile"))
    placed = (
        split_rows, split_rows, split_columns, split_flat, split_flat, split_flat,
        split_columns, split_flat, split_flat, split_flat,
        P(("groups", "tile"), None, None),
    ) + (P(),) * 12
    return jax.shard_map(
        body, mesh=mesh, in_specs=placed, out_specs=split_rows, check_vma=False
    )
```

```python
import functools

import jax
import jax.numpy as jnp
from jax import lax
from jax.experimental import pallas as pl
from jax.experimental.pallas import tpu as pltpu
from jax.sharding import PartitionSpec as P

HALO = 256
BLOCK = 512
LANES = 128
SPARE = 64
F32, BF16 = jnp.float32, jnp.bfloat16
NN = (((1,), (0,)), ((), ()))
NT = (((1,), (1,)), ((), ()))
TN = (((0,), (0,)), ((), ()))
TT = (((0,), (1,)), ((), ()))


def mul(a, b, dims=NN):
    return lax.dot_general(a, b, dims, preferred_element_type=F32)


def swish_of_half(half):
    return half * jnp.tanh(half) + half


def norm(x, axis):
    size = x.shape[axis]
    centered = x - jnp.sum(x, axis=axis, keepdims=True) * (1.0 / size)
    variance = jnp.sum(centered * centered, axis=axis, keepdims=True) * (1.0 / size)
    return centered, lax.rsqrt(variance + 1e-05)


def places(rows, indices):
    at = lax.broadcasted_iota(jnp.int32, (rows, indices.shape[1]), 0).astype(jnp.int16)
    one, zero = jnp.array(1, BF16), jnp.array(0, BF16)
    return jnp.where(at == indices.astype(jnp.int16), one, zero)


def split(x):
    high = x.astype(BF16)
    return high, (x - high.astype(F32)).astype(BF16)


def stack_feats(feats, w_feat, fa, wa):
    rows = feats.shape[0]
    fa[...] = jnp.zeros(fa.shape, F32)
    wa[...] = jnp.zeros(wa.shape, F32)
    f_high, f_low = split(feats[...])
    w_high, w_low = split(0.5 * w_feat[...])
    for at, (f, w) in enumerate(((f_high, w_high), (f_high, w_low), (f_low, w_high))):
        fa[at * rows : (at + 1) * rows, :] = f.astype(F32)
        wa[at * rows : (at + 1) * rows, :] = w.astype(F32)


def fetch(pairs, sems):
    copies = [pltpu.make_async_copy(a, b, sems.at[i]) for i, (a, b) in enumerate(pairs)]
    for copy in copies:
        copy.start()

    def ready(*which):
        for i in which:
            copies[i].wait()

    return ready


def summed_messages(total, pre_of, to_of, w_out, count):
    w_out = w_out[...]
    held = {}

    def first(i):
        return to_of(i), swish_of_half(pre_of(i)).astype(BF16)

    def second(i, to, hidden):
        return to, mul(w_out, hidden, TN)

    def third(i, to, out):
        one, part = out[:1, :], 1.0 / out.shape[0]
        moved = out - one
        mean = jnp.sum(moved, axis=0, keepdims=True) * part
        variance = jnp.sum(moved * moved, axis=0, keepdims=True) * part - mean * mean
        scale = lax.rsqrt(jnp.maximum(variance, 0.0) + 1e-05)
        live = lax.broadcasted_iota(jnp.int32, (1, BLOCK), 1) + i * BLOCK < count
        return to, ((out - (mean + one)) * jnp.where(live, scale, 0.0)).astype(BF16)

    def last(i, to, message):
        return (mul(to, message, NT),)

    stages = (first, second, third, last)
    summed = None
    for step in range(total // BLOCK + len(stages) - 1):
        for at, stage in enumerate(stages):
            i = step - at
            if 0 <= i < total // BLOCK:
                held[i] = stage(i, *held.get(i, ()))
                if stage is last:
                    part = held.pop(i)[0]
                    summed = part if summed is None else summed + part
    return summed.astype(BF16)


def nodes_of(latent, first, summed, w_in, w_out):
    hidden = swish_of_half(0.5 * (first + mul(summed, w_in))).astype(BF16)
    centered, scale = norm(mul(hidden, w_out[...]), 1)
    return (latent.astype(F32) + centered * scale).astype(BF16)


def in_a_column(asked):
    blocks, _, per = asked.shape
    size = (blocks, per, per)
    own = lax.broadcasted_iota(jnp.int32, size, 1) == lax.broadcasted_iota(jnp.int32, size, 2)
    column = jnp.sum(jnp.where(own, asked.astype(F32), 0.0), axis=2, keepdims=True)
    return column.reshape(blocks * per, 1).astype(jnp.int32)


def band_ends(
    grid_any, latent_any, feats_any, receiver_any,
    pair, other, middle, latent, feats, receiver, sems,
):
    last = grid_any.shape[0] - HALO
    first = (lax.axis_index("tile") % 2) * last
    pair_at, other_at = (pl.ds(pl.multiple_of(at, HALO), HALO) for at in (last - first, first))
    fetch(
        (
            (grid_any.at[pair_at, :], pair), (grid_any.at[other_at, :], other),
            (grid_any.at[HALO:last, :], middle), (latent_any, latent), (feats_any, feats),
            (receiver_any, receiver),
        ),
        sems,
    )(*range(6))


def encode(
    from_pair, from_other, pair, other, middle, latent, feats, receiver,
    count_any, sender_any, feat_any, recv_any, send_any, out_any, in_any, node_any, next_any,
    mid, sent,
    count, sender, w_feat, w_recv, w_send, w_out, w_in, w_node, w_next,
    first, table, picked, recv_table, fa, wa, sems,
):
    ready = fetch(
        (
            (sender_any, sender), (feat_any, w_feat), (recv_any, w_recv), (send_any, w_send),
            (out_any, w_out), (count_any, count), (in_any, w_in), (node_any, w_node),
            (next_any, w_next),
        ),
        sems,
    )
    own, width = middle.shape[0] + 2 * HALO, middle.shape[1]
    parts = width // LANES
    odd = lax.axis_index("tile") % 2 == 1

    def place_rows(at, rows):
        for c in range(parts):
            span = pl.ds(at * parts + c, rows.shape[0], stride=parts)
            table[span, :] = rows[:, c * LANES : (c + 1) * LANES].astype(F32)

    place_rows(2 * HALO, middle[...])
    place_rows(HALO, jnp.where(odd, pair[...], other[...]))
    place_rows(own, jnp.where(odd, other[...], pair[...]))
    place_rows(0, jnp.where(odd, from_pair[...], from_other[...]))
    place_rows(HALO + own, jnp.where(odd, from_other[...], from_pair[...]))
    ready(0, 1)

    def gather(i):
        for e in range(i * BLOCK, (i + 1) * BLOCK):
            row = table[pl.ds(sender[0, e] * parts, parts), :]
            picked[pl.ds(e // 8 * (8 * parts) + e % 8, parts, stride=8), :] = row

    gather(0)
    stack_feats(feats, w_feat, fa, wa)
    ready(2)
    recv_table[...] = (0.5 * mul(w_recv[...], latent[...], TT)).astype(BF16)
    wab = wa[...].astype(BF16)
    ready(3, 4, 5)
    half_send = w_send[...] * jnp.array(0.5, BF16)

    def to_of(i):
        return places(recv_table.shape[1], receiver[:, pl.ds(i * BLOCK, BLOCK)])

    def pre_of(i):
        span = pl.ds(i * BLOCK, BLOCK)
        size = BLOCK * parts
        rows = picked[i * size : (i + 1) * size, :].reshape(BLOCK // 8, parts, 8, LANES)
        rows = [rows[:, c].reshape(BLOCK, LANES).astype(BF16) for c in range(parts)]
        pre = mul(half_send, jnp.concatenate(rows, axis=1), TT)
        if (i + 1) * BLOCK < receiver.shape[1]:
            gather(i + 1)
        pre += mul(recv_table[...], to_of(i))
        return pre + mul(wab, fa[:, span].astype(BF16), TN)

    ready(6)
    first[...] = mul(latent[...], w_in[:width, :])
    summed = summed_messages(receiver.shape[1], pre_of, to_of, w_out, count[0])
    ready(7, 8)
    middle = nodes_of(latent[...], first[...], summed, w_in[width:, :], w_node)
    mid[...] = middle
    sent[...] = (0.5 * mul(middle, w_next[...])).astype(BF16)


def answer(sent, asked, outgoing_any, outgoing, sems):
    column = in_a_column(asked[...])
    size = (column.shape[0], sent.shape[0])
    at = (lax.broadcasted_iota(jnp.int32, size, 1) == column).astype(F32).astype(BF16)
    part = size[0] // sems.shape[0]
    copies = []
    for i in range(sems.shape[0]):
        span = pl.ds(i * part, part)
        outgoing[span, :] = mul(at[i * part : (i + 1) * part, :], sent[...]).astype(BF16)
        copies.append(
            pltpu.make_async_copy(outgoing.at[span, :], outgoing_any.at[span, :], sems.at[i])
        )
        copies[-1].start()
    for copy in copies:
        copy.wait()


def process_own(
    mid, feats_any, sender_any, receiver_any, feat_any, recv_any, in_any, out_any,
    pre, sender, receiver, w_out, first_any,
    feats, w_feat, w_recv, w_in, first, recv_table, fa, wa, sems, out_sems,
):
    ready = fetch(
        (
            (feats_any, feats), (feat_any, w_feat), (recv_any, w_recv), (receiver_any, receiver),
            (in_any.at[: w_in.shape[0], :], w_in), (out_any, w_out), (sender_any, sender),
        ),
        sems,
    )
    ready(0, 1)
    stack_feats(feats, w_feat, fa, wa)
    ready(2)
    recv_table[...] = (0.5 * mul(w_recv[...], mid[...], TT)).astype(BF16)
    wab = wa[...].astype(BF16)
    ready(3)
    for start in range(0, pre.shape[1], BLOCK):
        span = pl.ds(start, BLOCK)
        part = mul(recv_table[...], places(recv_table.shape[1], receiver[:, span]))
        pre[:, span] = (part + mul(wab, fa[:, span].astype(BF16), TN)).astype(pre.dtype)
    ready(4)
    first[...] = mul(mid[...], w_in[...])
    fetch(((first, first_any),), out_sems)(0)
    ready(5, 6)


def process_rest(
    count, mid, pre, sender, receiver, listed, w_out, first_any, in_any, node_any,
    result_any,
    first, w_in, w_node, result, sems, out_sems,
):
    ready = fetch(
        (
            (first_any, first), (in_any.at[w_in.shape[0] :, :], w_in), (node_any, w_node),
        ),
        sems,
    )
    table = listed[...].T

    def to_of(i):
        return places(mid.shape[0], receiver[:, pl.ds(i * BLOCK, BLOCK)])

    def pre_of(i):
        span = pl.ds(i * BLOCK, BLOCK)
        return pre[:, span] + mul(table, places(table.shape[1], sender[:, span]))

    summed = summed_messages(sender.shape[1], pre_of, to_of, w_out, count[0])
    ready(0, 1, 2)
    result[...] = nodes_of(mid[...], first[...], summed, w_in[...], w_node)
    fetch(((result, result_any),), out_sems)(0)


S, V, H = (pl.BlockSpec(memory_space=m) for m in (pltpu.SMEM, pltpu.VMEM, pltpu.HBM))


class Scalars(jax.ShapeDtypeStruct):
    pass


def shape(*sizes, dtype=BF16):
    return jax.ShapeDtypeStruct(sizes, dtype)


def call(kernel, name, near, far, near_outs, far_outs, scratch, copies, counts=()):
    return pl.pallas_call(
        kernel,
        out_shape=near_outs + far_outs,
        in_specs=[S] * len(counts) + [V] * len(near) + [H] * len(far),
        out_specs=[V] * len(near_outs) + [H] * len(far_outs),
        scratch_shapes=[
            (pltpu.SMEM if isinstance(s, Scalars) else pltpu.VMEM)(s.shape, s.dtype)
            for s in scratch
        ]
        + [pltpu.SemaphoreType.DMA((n,)) for n in copies],
        compiler_params=pltpu.CompilerParams(vmem_limit_bytes=48 * 2**20),
        name=name,
    )(*counts, *near, *(x if x.size == 1 else pltpu.with_memory_space_constraint(x, pltpu.HBM) for x in far))


def body(
    grid_latent, mesh_latent, enc_feats, enc_sender, enc_receiver, enc_count,
    mesh_feats, mesh_sender, mesh_receiver, mesh_count, need_rows,
    w_enc_feat, w_enc_send, w_enc_recv, w_enc_out, w_enc_node_in, w_enc_node_out,
    w_proc_feat, w_proc_send, w_proc_recv, w_proc_out, w_proc_node_in, w_proc_node_out,
):
    nodes, width = mesh_latent.shape
    rows = grid_latent.shape[0]
    slots = enc_feats.shape[1]
    blocks = lax.axis_size("tile")
    per = need_rows.shape[2]
    square = shape(width, width)
    one, scalars = (Scalars(n, jnp.int32) for n in ((1,), (1, slots)))
    node_rows = shape(nodes, width)
    edge_index = shape(1, slots, dtype=jnp.int32)
    edge_feats = shape(*enc_feats.shape, dtype=F32)
    feat_weight = shape(*w_enc_feat.shape, dtype=F32)
    stacked = [shape(16, slots, dtype=F32), shape(16, width, dtype=F32)]
    enc_sender, enc_receiver, mesh_sender, mesh_receiver = (
        x.reshape(1, slots) for x in (enc_sender, enc_receiver, mesh_sender, mesh_receiver)
    )

    asked = lax.all_to_all(
        need_rows.reshape(blocks, 1, per), "tile", split_axis=0, concat_axis=0, tiled=True
    )
    near = call(
        band_ends,
        "band_ends",
        [],
        [grid_latent, mesh_latent, enc_feats, enc_receiver],
        [
            shape(HALO, width), shape(HALO, width), shape(rows - 2 * HALO, width), node_rows,
            edge_feats, edge_index,
        ],
        [],
        [],
        (6,),
    )
    for_pair, for_other = near[:2]
    pairs = [(i, i ^ 1) for i in range(blocks)]
    others = [(i, i + 1 if i % 2 else i - 1) for i in range(1, blocks - 1)]
    from_pair = lax.ppermute(for_pair, "tile", pairs)
    from_other = lax.ppermute(for_other, "tile", others)
    mid, sent = call(
        encode,
        "encode",
        [from_pair, from_other, *near],
        [
            enc_count, enc_sender, w_enc_feat, w_enc_recv, w_enc_send, w_enc_out, w_enc_node_in,
            w_enc_node_out, w_proc_send,
        ],
        [node_rows, node_rows],
        [],
        [
            one, scalars, feat_weight, square, square, square, shape(2 * width, width), square,
            square,
            shape(nodes, width, dtype=F32),
            shape((rows + 2 * HALO) * width // LANES + SPARE, LANES, dtype=F32),
            shape(slots * width // LANES + SPARE, LANES, dtype=F32), shape(width, nodes),
        ]
        + stacked,
        (9,),
    )
    (outgoing,) = call(
        answer,
        "answer",
        [sent, asked],
        [],
        [],
        [shape(blocks * per, width)],
        [shape(blocks * per, width)],
        (2,),
    )
    listed = lax.all_to_all(
        outgoing.reshape(blocks, per, width), "tile", split_axis=0, concat_axis=0, tiled=True
    ).reshape(blocks * per, width)
    pre, near_sender, near_receiver, w_out, first = call(
        process_own,
        "process_own",
        [mid],
        [
            mesh_feats, mesh_sender, mesh_receiver, w_proc_feat, w_proc_recv, w_proc_node_in,
            w_proc_out,
        ],
        [shape(width, slots), edge_index, edge_index, square],
        [shape(nodes, width, dtype=F32)],
        [
            edge_feats, feat_weight, square, square, shape(nodes, width, dtype=F32),
            shape(width, nodes),
        ]
        + stacked,
        (7, 1),
    )
    (result,) = call(
        process_rest,
        "process_rest",
        [mid, pre, near_sender, near_receiver, listed, w_out],
        [first, w_proc_node_in, w_proc_node_out],
        [],
        [node_rows],
        [
            shape(nodes, width, dtype=F32), square, square, node_rows,
        ],
        (3, 1),
        [mesh_count],
    )
    return result


def solution(mesh):
    split_rows = P(("groups", "tile"), None)
    split_columns = P(None, ("groups", "tile"))
    split_flat = P(("groups", "tile"))
    placed = (
        split_rows, split_rows, split_columns, split_flat, split_flat, split_flat,
        split_columns, split_flat, split_flat, split_flat,
        P(("groups", "tile"), None, None),
    ) + (P(),) * 12
    return jax.shard_map(
        body, mesh=mesh, in_specs=placed, out_specs=split_rows, check_vma=False
    )
```
